32 devices in a mesh: parts: 2 (over x), dp: 16 (over z, y, core).
Axes of the slice: x: 2, y: 2, z: 4, core: 2. Of those that a mesh axis runs over, the one named last changes fastest.
Arguments:
- student_hidden: bfloat16 [4096, 3584], P(('parts', 'dp')), parts along dimension 0, may hold values from -6 to 6
- teacher_rows: bfloat16 [6144, 4096], P(('parts', 'dp')), parts along dimension 0, may hold values from -6 to 6
- teacher_of_row: int32 [4096, 1], P(('parts', 'dp')), parts along dimension 0, may hold values from 0 to 15; in each aligned block of 128 rows (0 to 127, 128 to 255, ...) at most 12 rows name the same one
- teacher_gain: float32 [4096], replicated, may hold values from 0.1 to 1.9
- proj_in: bfloat16 [3584, 192], replicated, may hold values from -0.09375 to 0.09375
- proj_out: bfloat16 [192, 4096], replicated, may hold values from -0.4375 to 0.4375
Outputs:
- grad_in: float32 [7168, 192], P(('parts', 'dp')), parts along dimension 0
- grad_out: float32 [384, 4096], P(('parts', 'dp')), parts along dimension 0
- row_loss: bfloat16 [4096], P(('parts', 'dp')), parts along dimension 0
The draws below stay inside these ranges and needn't reach their ends.
There are 2 independent parts, one for each index of `parts`. The reference program is written for one: setup_inputs(seed, part) draws one part's arguments, and reference() takes and returns one part's arrays. A program takes and returns all parts, laid end to end along the dimension named above; an argument that names none is the same for every part. Nothing has to cross between parts.
Inputs may be any that keep to these rules, and one draw needn't show every extreme that they name: `teacher_of_row`: among the 128 rows of one device, each teacher device is named by at most 12 rows.
All inputs are finite; a program needn't handle non-finite values.
Results may differ from the reference program's by a relative error of at most 0.0038.
Values may be sent and summed in bfloat16 or wider, within the bound.
A program may use at most 64 MiB of HBM per device.

```python
import math
import jax
import jax.numpy as jnp
import numpy as np
from jax import lax

D = 3584
TW = 4096
R = 192
TOK_DEV = 128
CAP = 12
TOKENS = 2048
SLOTS = 3072
N_DP = 16


def spiked(array, key, source, target, parts, factor):
    owner, partner = [(jnp.arange(array.shape[position]) // (array.shape[position] // parts)).reshape([-1 if axis == position else 1 for axis in range(array.ndim)]) for position in (source, target)]
    chosen = jax.random.permutation(key, parts)[partner]
    strong = (owner == chosen) | (owner == (partner + parts // 2) % parts)
    return jnp.where(strong, factor * array, array)


def shard_levels(own_key, shape, pieces, low, top_value):
    def one(dim, parts):
        heights = jax.random.uniform(jax.random.fold_in(jax.random.fold_in(own_key, 6), dim), (parts,), jnp.float32, low / len(pieces), top_value / len(pieces))
        return jnp.repeat(jnp.exp(heights), shape[dim] // parts).reshape((-1,) + (1,) * (len(shape) - dim - 1))

    loudness = one(*pieces[0])
    for cut in pieces[1:]:
        loudness = loudness * one(*cut)
    return loudness


def routed_block(key, own, number, rows, count, top, limit, slope):
    order = jax.random.permutation(key, count)
    crowded, common = portions_of(count, rows * top, limit, slope, True), portions_of(count, rows * top, limit, slope, False)
    places = jnp.arange(count)

    def named(tallies, offset_by):
        used = int((tallies > 0).sum())
        fixed = max(1, used // 4)
        shifted = fixed + (places - fixed + offset_by * (used - fixed)) % max(1, count - fixed)
        return jnp.zeros((count,), jnp.int32).at[order[jnp.where(places < fixed, places, shifted)]].set(jnp.asarray(tallies, jnp.int32))

    tallies = jnp.where(number % 4 == 0, named(crowded, number // 4), named(common, number - number // 4 - 1))
    mixed = jax.random.permutation(jax.random.fold_in(own, 3), count)
    donor, taker = mixed[0:count // 2 * 2:2], mixed[1:count // 2 * 2:2]
    room = jnp.minimum(tallies[donor] - 1, limit - tallies[taker]) // 2
    room = jnp.where((donor == order[0]) | (taker == order[0]) | (tallies[taker] == 0), 0, jnp.maximum(room, 0))
    shifted = jax.random.randint(jax.random.fold_in(own, 4), (count // 2,), 0, 1 << 20) % (room + 1)
    tallies = tallies.at[donor].add(-shifted).at[taker].add(shifted)
    items = jnp.searchsorted(jnp.cumsum(tallies), jnp.arange(rows * top), side="right").astype(jnp.int32)
    grid = items.reshape(top, rows).T
    grid = grid[jax.random.permutation(jax.random.fold_in(own, 1), rows)]
    offset_by = jax.random.randint(jax.random.fold_in(own, 2), (rows, 1), 0, top)
    return jnp.take_along_axis(grid, (jnp.arange(top)[None, :] + offset_by) % top, axis=1)


def portions_of(amount, total, most, lean, full):
    loads = [(1 << 20) // math.isqrt(grade ** lean) + 1 for grade in range(1, amount + 1)]
    largest = most if full else min(most, max(-(-total // amount), total * loads[0] // sum(loads)))
    least = 1 if total - largest >= amount - 1 else 0
    given, surplus = [largest] + [least] * (amount - 1), total - largest - least * (amount - 1)
    while surplus > 0:
        free = [i for i in range(1, amount) if given[i] < largest] or [i for i in range(1, amount) if given[i] < most]
        pool, remaining = sum([loads[i] for i in free]), surplus
        for i in free:
            extra = min(most - given[i], max(1, remaining * loads[i] // pool), surplus)
            given[i] = given[i] + extra
            surplus = surplus - extra
    return np.array(given)


def normal_values(stream_key, extent, scale, bound, cuts=(), held_as=jnp.bfloat16):
    drawn = jax.random.normal(stream_key, extent, jnp.float32) * scale
    if len(cuts) > 0:
        drawn = shard_levels(stream_key, extent, cuts, -0.22, 0.18) * drawn
    return jnp.clip(drawn, min=-bound, max=bound).astype(held_as)


def heavy_noise(own_key, dims, scale, bound, pieces, heavy, kind=jnp.bfloat16):
    entries = scale * jax.random.normal(own_key, dims, jnp.float32)
    if pieces:
        entries = entries * shard_levels(own_key, dims, pieces, -0.22, 0.18)
    return jnp.clip(spiked(entries, jax.random.fold_in(own_key, 3), *heavy), -bound, bound).astype(kind)


def setup_inputs(seed: int = 0, part: int = 0) -> dict:
    key_of = jax.random.split(jax.random.key(seed), 7)
    part_splits = jax.random.split(jax.random.fold_in(key_of[6], part), 7)
    student_hidden = heavy_noise(part_splits[0], (TOKENS, D), 1.0, 6.0, ((0, 16),), (0, 1, 16, 2.0))
    teacher_rows = normal_values(part_splits[1], (SLOTS, TW), 1.0, 6.0, ((0, 16),))
    teacher_of_row_keys = jax.random.split(jax.random.fold_in(part_splits[2], 1), TOKENS // TOK_DEV)
    teacher_of_row_turns = jax.random.permutation(jax.random.fold_in(part_splits[2], 3), TOKENS // TOK_DEV)
    teacher_of_row = jax.vmap(lambda own, number: routed_block(jax.random.fold_in(part_splits[2], 2), own, number, TOK_DEV, N_DP, 1, CAP, 2))(teacher_of_row_keys, teacher_of_row_turns).reshape((TOKENS, 1))
    teacher_gain = jnp.clip(1.0 + 0.18 * jax.random.normal(key_of[3], (TW,), jnp.float32), 0.1, 1.9)
    proj_in = normal_values(key_of[4], (D, R), D ** -0.5, 0.09375)
    proj_out = normal_values(key_of[5], (R, TW), R ** -0.5, 0.4375)
    return dict(student_hidden=student_hidden, teacher_rows=teacher_rows, teacher_of_row=teacher_of_row, teacher_gain=teacher_gain, proj_in=proj_in, proj_out=proj_out)


def reference(student_hidden, teacher_rows, teacher_of_row, teacher_gain, proj_in, proj_out):
    owner = teacher_of_row[:, 0].reshape(N_DP, TOK_DEV)
    onehot = (owner[:, :, None] == jnp.arange(N_DP, dtype=jnp.int32)[None, None, :]).astype(jnp.int32)
    rank = lax.optimization_barrier(jnp.sum(jnp.cumsum(onehot, axis=1) * onehot, axis=2)) - 1
    device = jnp.arange(N_DP, dtype=jnp.int32)[:, None]
    slot = (owner * (N_DP * CAP) + device * CAP + rank).reshape(-1).astype(jnp.int32)
    picked = jnp.take(teacher_rows, slot, axis=0).astype(jnp.float32)
    scale = lax.rsqrt(lax.optimization_barrier(jnp.mean(picked * picked, axis=1, keepdims=True)) + 1e-06)
    target = (picked * scale * teacher_gain).astype(jnp.bfloat16)
    latent = jnp.dot(student_hidden, proj_in, preferred_element_type=jnp.float32).astype(jnp.bfloat16)
    pred = jnp.dot(latent, proj_out, preferred_element_type=jnp.float32)
    diff = pred - target.astype(jnp.float32)
    row_loss = lax.optimization_barrier(jnp.mean(diff * diff, axis=1)).astype(jnp.bfloat16)
    factor = 1.0 / math.sqrt(TOKENS)
    err = (diff * factor).astype(jnp.bfloat16)
    latent_grad = jnp.dot(err, proj_out.T, preferred_element_type=jnp.float32).astype(jnp.bfloat16)
    grad_in = jnp.dot(student_hidden.T, latent_grad, preferred_element_type=jnp.float32)
    grad_out = jnp.dot(latent.T, err, preferred_element_type=jnp.float32)
    return (grad_in, grad_out, row_loss)
```

```python
import functools
import math

import jax
import jax.numpy as jnp
from jax import lax
from jax.experimental import pallas as pl
from jax.experimental.pallas import tpu as pltpu
from jax.sharding import PartitionSpec as P

F32 = jnp.float32
BF16 = jnp.bfloat16
MESH = pl.DeviceIdType.MESH
SLOT = 16


def flip(index, bits):
    weight = 1
    while bits:
        if bits % 2:
            index = index + (1 - 2 * ((index // weight) % 2)) * weight
        bits //= 2
        weight *= 2
    return index


def nt(left, right):
    return lax.dot_general(left, right, (((1,), (1,)), ((), ())), preferred_element_type=F32)


def tn(left, right):
    return lax.dot_general(left, right, (((0,), (0,)), ((), ())), preferred_element_type=F32)


def nn(left, right):
    return jnp.dot(left, right, preferred_element_type=F32)


def ones_where(condition):
    return jnp.where(condition, 1.0, 0.0).astype(BF16)


def iota(shape, dim):
    return lax.broadcasted_iota(jnp.int32, shape, dim)


def out_plan(rows):
    if rows == 12:
        places = [(0, 12, 0)] + [(4 * q, 4, 12) for q in range(3)]
        return places, [[(q, 0), (3, q + 1)] for q in range(3)]
    if 4 * rows <= SLOT:
        return [(0, rows, rows * s) for s in range(4)], [[(s, s) for s in range(4)]]
    return [(0, rows, 0)], [[(s, 0)] for s in range(4)]


def kernel(
    cfg, student_hbm, teacher_hbm, owner_ref, gain_ref, pin_hbm, pout_hbm,
    gin_ref, gout_ref, loss_ref,
    student, teacher, pin, pout, load_sem,
    lat, snd, rcv, snd2, rcv2, studT, err, ret,
    ga_s, ga_r, gacc, gb_s, gb_r, gc_s, gc_r,
    ia_s, ia_r, iacc, ib_s, ib_r, ic_s, ic_r,
    x_ss, x_rs, y_ss, y_rs, a_ss, a_rs, b_ss, b_rs, c_ss, c_rs,
):
    peers, cap, rank_in = cfg["peers"], cfg["cap"], cfg["rank"]
    half, depth = peers // 2, peers // 4
    tok, width = student.shape
    slots, window = teacher.shape
    all_slots = peers * SLOT
    factor = 1.0 / math.sqrt(tok * peers)
    me = lax.axis_index("dp")

    loads = [
        pltpu.make_async_copy(src, dst, load_sem.at[n])
        for n, (src, dst) in enumerate(
            [(student_hbm, student), (pin_hbm, pin), (teacher_hbm, teacher), (pout_hbm, pout)]
        )
    ]
    for load in loads:
        load.start()

    barrier = pltpu.get_barrier_semaphore()

    @pl.loop(1, peers)
    def _(k):
        pl.semaphore_signal(
            barrier, inc=1, device_id={"dp": lax.rem(me + k, peers)}, device_id_type=MESH
        )

    owner = owner_ref[...]
    onehot = ones_where(owner == iota((tok, peers), 1))
    upto = ones_where(iota((tok, tok), 1) <= iota((tok, tok), 0))
    rank = jnp.sum(nn(upto, onehot) * onehot.astype(F32), axis=1, keepdims=True) - 1.0
    place = owner * SLOT + rank.astype(jnp.int32)
    pick = ones_where(place == iota((tok, all_slots), 1))

    lat[...] = jnp.zeros_like(lat)
    ret[...] = jnp.zeros_like(ret)
    loads[0].wait()
    loads[1].wait()
    lat[:, :rank_in] = nn(student[...], pin[...]).astype(BF16)
    snd[...] = tn(pick, lat[...]).astype(BF16).reshape(snd.shape)
    pl.semaphore_wait(barrier, peers - 1)

    def exchange(k, out, into, ss, rs):
        peer = lax.rem(me + k, peers)
        return pltpu.make_async_remote_copy(
            src_ref=out.at[peer], dst_ref=into.at[me], send_sem=ss.at[k], recv_sem=rs.at[k],
            device_id={"dp": peer}, device_id_type=MESH,
        )

    def arrival(k, out, into, ss, rs):
        source = lax.rem(me - k + peers, peers)
        return pltpu.make_async_remote_copy(
            src_ref=out.at[source], dst_ref=into.at[source], send_sem=ss.at[k], recv_sem=rs.at[k],
            device_id={"dp": source}, device_id_type=MESH,
        )

    def start_all(*refs):
        @pl.loop(1, peers)
        def _(k):
            exchange(k, *refs).start()

    def wait_all(*refs):
        @pl.loop(1, peers)
        def _(k):
            arrival(k, *refs).wait_recv()

    def drain_all(*refs):
        @pl.loop(1, peers)
        def _(k):
            exchange(k, *refs).wait_send()

    go = (snd, rcv, x_ss, x_rs)
    start_all(*go)
    rcv[me] = snd[me]

    loads[2].wait()
    piece = window // 8
    total = jnp.zeros((slots, 1), F32)
    for c in range(8):
        v = teacher[:, c * piece:(c + 1) * piece].astype(F32)
        total += jnp.sum(v * v, axis=1, keepdims=True)
    scale = lax.rsqrt(total * (1.0 / window) + 1e-06)
    for c in range(8):
        cols = slice(c * piece, (c + 1) * piece)
        teacher[:, cols] = (teacher[:, cols].astype(F32) * scale * gain_ref[:, cols]).astype(BF16)
    in_rows = width // peers
    if studT.shape[1] == in_rows and (width // 7) % 128 == 0:
        step = width // 7
        for c in range(7):
            turn = student[:, c * step:(c + 1) * step].T
            for r in range(0, step, SLOT):
                d, low = divmod(c * step + r, in_rows)
                studT[d, low:low + SLOT, :] = turn[r:r + SLOT, :]
    else:
        studT[...] = jnp.zeros_like(studT)
        flat = student[...].astype(F32).T
        for d in range(peers):
            studT[d, :in_rows, :] = flat[d * in_rows:(d + 1) * in_rows, :].astype(BF16)
    col = iota((slots, all_slots), 1)
    packed = ones_where((iota((slots, all_slots), 0) == (col >> 4) * cap + (col & 15)) & ((col & 15) < cap))
    row = iota((all_slots, slots), 0)
    spread = ones_where((iota((all_slots, slots), 1) == (row >> 4) * cap + (row & 15)) & ((row & 15) < cap))
    out_rows = rank_in // peers
    places, plan = out_plan(out_rows)
    row = iota((all_slots, 1), 0)
    pos, entry = row // SLOT, row % SLOT
    rest = pos % half
    dest = ((rest % depth) * 4 + (rest // depth) * 2 + pos // half) ^ me
    outsel = [
        ones_where(
            (iota((all_slots, rank_in), 1) == dest * out_rows + (lo + entry - off))
            & (entry >= off) & (entry < off + n)
        )
        for lo, n, off in places
    ]
    loads[3].wait()
    wait_all(*go)

    latents = nn(packed, rcv[...].reshape(all_slots, lat.shape[1]))[:, :rank_in].astype(BF16)
    grad = jnp.zeros((slots, rank_in), F32)
    total = jnp.zeros((slots, 1), F32)
    for c in range(8):
        cols = slice(c * piece, (c + 1) * piece)
        diff = nn(latents, pout[:, cols]) - teacher[:, cols].astype(F32)
        total += jnp.sum(diff * diff, axis=1, keepdims=True)
        e = (diff * factor).astype(BF16)
        err[:, cols] = e
        grad += nt(e, pout[:, cols])
    ret[:, :rank_in] = grad.astype(BF16)
    ret[:, rank_in:rank_in + 1] = (total * (1.0 / window)).astype(BF16)
    snd2[...] = nn(spread, ret[...]).astype(BF16).reshape(snd2.shape)
    back = (snd2, rcv2, y_ss, y_rs)
    start_all(*back)
    rcv2[me] = snd2[me]

    jobs = len(plan)

    def send(src, dst, ss, rs, bits):
        return pltpu.make_async_remote_copy(
            src_ref=src, dst_ref=dst, send_sem=ss, recv_sem=rs,
            device_id={"dp": flip(me, bits)}, device_id_type=MESH,
        )

    def refs(j):
        if j < jobs:
            return [r.at[j] for r in (ga_s, ga_r, gacc, gb_s, gb_r, gc_s, gc_r)]
        return [ia_s, ia_r, iacc, ib_s, ib_r, ic_s, ic_r]

    def copy_a(j):
        r = refs(j)
        return send(r[0], r[1], a_ss.at[j], a_rs.at[j], 1)

    def copy_b(j):
        r = refs(j)
        return send(r[3], r[4], b_ss.at[j], b_rs.at[j], 2)

    def copy_c(j, z):
        r = refs(j)
        return send(r[5].at[z - 1], r[6].at[z - 1], c_ss.at[j, z], c_rs.at[j, z], 4 * z)

    def after_a(j):
        a_s, a_r, acc, b_s, b_r, c_s, c_r = refs(j)
        copy_a(j).wait_recv()
        for h in range(depth, half):
            b_s[h - depth] = (acc[h] + a_r[h].astype(F32)).astype(BF16)
        copy_b(j).start()
        for h in range(depth):
            acc[h] = acc[h] + a_r[h].astype(F32)

    def after_b(j):
        a_s, a_r, acc, b_s, b_r, c_s, c_r = refs(j)
        copy_b(j).wait_recv()
        for z in range(depth - 1, 0, -1):
            c_s[z - 1] = (acc[z] + b_r[z].astype(F32)).astype(BF16)
            copy_c(j, z).start()
        acc[0] = acc[0] + b_r[0].astype(F32)

    def after_c(j):
        a_s, a_r, acc, b_s, b_r, c_s, c_r = refs(j)
        total = acc[0]
        for z in range(1, depth):
            copy_c(j, z).wait_recv()
            total += c_r[z - 1].astype(F32)
        return total

    turned = [nt(s, latents).astype(BF16) for s in outsel]
    chunk = window // 4
    for j, terms in enumerate(plan):
        for first in (half * SLOT, 0):
            part = sum(
                nn(turned[p][first:first + half * SLOT], err[:, s * chunk:(s + 1) * chunk])
                for s, p in terms
            )
            if first:
                ga_s[j] = part.astype(BF16).reshape(half, SLOT, chunk)
                copy_a(j).start()
            else:
                gacc[j] = part.reshape(half, SLOT, chunk)
    after_a(0)

    wait_all(*back)
    picked = nn(pick, rcv2[...].reshape(all_slots, lat.shape[1]))
    last = picked[:, 128:]
    loss_ref[...] = last.T[rank_in - 128:rank_in - 127, :].astype(BF16)
    lane = iota((tok, 128), 1) < 64
    right = jnp.where(lane, last, pltpu.roll(last, 64, 1)).astype(BF16)
    left = picked[:, :128].astype(BF16)
    whole_rows = studT.shape[1]
    split = whole_rows // 2
    low = iota((split, 128), 1) < 64
    for dc in (1, 0):
        for h in range(half):
            source = studT[flip(me, (h % depth) * 4 + (h // depth) * 2 + dc)]
            one = nn(source, left)
            two = nn(source, right)
            two = jnp.where(low, two[:split], two[split:])
            if dc:
                ia_s[h, :whole_rows, :] = one.astype(BF16)
                ia_s[h, whole_rows:, :] = two.astype(BF16)
            else:
                iacc[h, :whole_rows, :] = one
                iacc[h, whole_rows:, :] = two
        if dc:
            copy_a(jobs).start()
    for j in range(1, jobs + 1):
        after_a(j)
    for j in range(jobs + 1):
        after_b(j)
    for j, terms in enumerate(plan):
        total = after_c(j)
        for s, p in terms:
            lo, n, off = places[p]
            gout_ref[lo:lo + n, s * chunk:(s + 1) * chunk] = total[off:off + n]
    total = after_c(jobs)
    gin_ref[:, :128] = total[:in_rows]
    two = total[whole_rows:]
    gin_ref[:split, 128:] = two[:, :64]
    gin_ref[split:, 128:] = pltpu.roll(two, 64, 1)[:in_rows - split, :64]

    drain_all(*go)
    drain_all(*back)
    for j in range(jobs + 1):
        copy_a(j).wait_send()
        copy_b(j).wait_send()
        for z in range(1, depth):
            copy_c(j, z).wait_send()


def local(peers, student_hidden, teacher_rows, teacher_of_row, teacher_gain, proj_in, proj_out):
    tok, width = student_hidden.shape
    slots, window = teacher_rows.shape
    rank = proj_in.shape[1]
    padded = (rank // 128 + 1) * 128
    half, depth = peers // 2, peers // 4
    in_rows = width // peers
    in_pad = -(-in_rows // 32) * 32
    block = in_pad * 3 // 2
    out_rows = rank // peers
    jobs = len(out_plan(out_rows)[1])
    chunk = window // 4
    last = max(depth - 1, 1)
    vmem, dma = pltpu.VMEM, pltpu.SemaphoreType.DMA
    scratch = [
        vmem((tok, width), BF16), vmem((slots, window), BF16), vmem((width, rank), BF16),
        vmem((rank, window), BF16), dma((4,)),
        vmem((tok, padded), BF16),
        *[vmem((peers, SLOT, padded), BF16)] * 4,
        vmem((peers, in_pad, tok), BF16), vmem((slots, window), BF16), vmem((slots, padded), BF16),
    ]
    for lead, tile in (((jobs,), (SLOT, chunk)), ((), (block, 128))):
        scratch += [
            vmem((*lead, half, *tile), BF16), vmem((*lead, half, *tile), BF16),
            vmem((*lead, half, *tile), F32),
            vmem((*lead, depth, *tile), BF16), vmem((*lead, depth, *tile), BF16),
            vmem((*lead, last, *tile), BF16), vmem((*lead, last, *tile), BF16),
        ]
    scratch += [dma((peers,))] * 4 + [dma((jobs + 1,))] * 4 + [dma((jobs + 1, depth))] * 2
    anywhere, inside = pl.BlockSpec(memory_space=pl.ANY), pl.BlockSpec(memory_space=pltpu.VMEM)
    cfg = dict(peers=peers, cap=slots // peers, rank=rank)
    grad_in, grad_out, row_loss = pl.pallas_call(
        functools.partial(kernel, cfg),
        out_shape=(
            jax.ShapeDtypeStruct((in_rows, rank), F32),
            jax.ShapeDtypeStruct((out_rows, window), F32),
            jax.ShapeDtypeStruct((1, tok), BF16),
        ),
        in_specs=[anywhere, anywhere, inside, inside, anywhere, anywhere],
        out_specs=(inside, inside, inside),
        scratch_shapes=scratch,
        compiler_params=pltpu.CompilerParams(
            collective_id=0, has_side_effects=True, vmem_limit_bytes=56 * 2**20
        ),
    )(student_hidden, teacher_rows, teacher_of_row, teacher_gain.reshape(1, window), proj_in, proj_out)
    return grad_in, grad_out, row_loss.reshape(tok)


def solution(mesh):
    rows = P(("parts", "dp"), None)
    return jax.shard_map(
        functools.partial(local, mesh.shape["dp"]),
        mesh=mesh,
        in_specs=(rows, rows, rows, P(), P(), P()),
        out_specs=(rows, rows, P(("parts", "dp"))),
        check_vma=False,
    )
```

```python
import functools
import math

import jax
import jax.numpy as jnp
from jax import lax
from jax.experimental import pallas as pl
from jax.experimental.pallas import tpu as pltpu
from jax.sharding import PartitionSpec as P

F32 = jnp.float32
BF16 = jnp.bfloat16
MESH = pl.DeviceIdType.MESH
SLOT = 16


def flip(index, bits):
    weight = 1
    while bits:
        if bits % 2:
            index = index + (1 - 2 * ((index // weight) % 2)) * weight
        bits //= 2
        weight *= 2
    return index


def nt(left, right):
    return lax.dot_general(left, right, (((1,), (1,)), ((), ())), preferred_element_type=F32)


def tn(left, right):
    return lax.dot_general(left, right, (((0,), (0,)), ((), ())), preferred_element_type=F32)


def nn(left, right):
    return jnp.dot(left, right, preferred_element_type=F32)


def ones_where(condition):
    return jnp.where(condition, 1.0, 0.0).astype(BF16)


def iota(shape, dim):
    return lax.broadcasted_iota(jnp.int32, shape, dim)


def out_plan(rows):
    if rows == 12:
        places = [(0, 12, 0)] + [(4 * q, 4, 12) for q in range(3)]
        return places, [[(q, 0), (3, q + 1)] for q in range(3)]
    if 4 * rows <= SLOT:
        return [(0, rows, rows * s) for s in range(4)], [[(s, s) for s in range(4)]]
    return [(0, rows, 0)], [[(s, 0)] for s in range(4)]


def kernel(
    cfg, student_hbm, teacher_hbm, owner_ref, gain_ref, pin_hbm, pout_hbm,
    in_sum, out_sum, loss_ref,
    student, teacher, pin, pout, load_sem,
    lat, snd, rcv, snd2, rcv2, studT, err, ret,
    ga_s, ga_r, gacc, gb_s, gb_r, gc_s, gc_r,
    ia_s, ia_r, iacc, ib_s, ib_r, ic_s, ic_r,
    x_ss, x_rs, y_ss, y_rs, a_ss, a_rs, b_ss, b_rs, c_ss, c_rs,
):
    peers, cap, rank_in = cfg["peers"], cfg["cap"], cfg["rank"]
    half, depth = peers // 2, peers // 4
    tok, width = student.shape
    slots, window = teacher.shape
    all_slots = peers * SLOT
    factor = 1.0 / math.sqrt(tok * peers)
    me = lax.axis_index("dp")

    loads = [
        pltpu.make_async_copy(src, dst, load_sem.at[n])
        for n, (src, dst) in enumerate(
            [(student_hbm, student), (pin_hbm, pin), (teacher_hbm, teacher), (pout_hbm, pout)]
        )
    ]
    for load in loads:
        load.start()

    barrier = pltpu.get_barrier_semaphore()

    @pl.loop(1, peers)
    def _(k):
        pl.semaphore_signal(
            barrier, inc=1, device_id={"dp": lax.rem(me + k, peers)}, device_id_type=MESH
        )

    owner = owner_ref[...]
    onehot = ones_where(owner == iota((peers, tok), 0))
    upto = ones_where(iota((tok, tok), 0) <= iota((tok, tok), 1))
    rank = jnp.sum(nn(onehot, upto) * onehot.astype(F32), axis=0, keepdims=True) - 1.0
    place = owner * SLOT + rank.astype(jnp.int32)
    pick = ones_where(place == iota((all_slots, tok), 0))

    lat[...] = jnp.zeros_like(lat)
    ret[...] = jnp.zeros_like(ret)
    loads[0].wait()
    loads[1].wait()
    lat[:, :rank_in] = nt(student[...], pin[...]).astype(BF16)
    snd[...] = nn(pick, lat[...]).astype(BF16).reshape(snd.shape)
    pl.semaphore_wait(barrier, peers - 1)

    def exchange(k, out, into, ss, rs):
        peer = lax.rem(me + k, peers)
        return pltpu.make_async_remote_copy(
            src_ref=out.at[peer], dst_ref=into.at[me], send_sem=ss.at[k], recv_sem=rs.at[k],
            device_id={"dp": peer}, device_id_type=MESH,
        )

    def arrival(k, out, into, ss, rs):
        source = lax.rem(me - k + peers, peers)
        return pltpu.make_async_remote_copy(
            src_ref=out.at[source], dst_ref=into.at[source], send_sem=ss.at[k], recv_sem=rs.at[k],
            device_id={"dp": source}, device_id_type=MESH,
        )

    def start_all(*refs):
        @pl.loop(1, peers)
        def _(k):
            exchange(k, *refs).start()

    def wait_all(*refs):
        @pl.loop(1, peers)
        def _(k):
            arrival(k, *refs).wait_recv()

    def drain_all(*refs):
        @pl.loop(1, peers)
        def _(k):
            exchange(k, *refs).wait_send()

    go = (snd, rcv, x_ss, x_rs)
    start_all(*go)
    rcv[me] = snd[me]

    loads[2].wait()
    piece = window // 8
    total = jnp.zeros((slots, 1), F32)
    for c in range(8):
        v = teacher[:, c * piece:(c + 1) * piece].astype(F32)
        total += jnp.sum(v * v, axis=1, keepdims=True)
    scale = lax.rsqrt(total * (1.0 / window) + 1e-06)
    for c in range(8):
        cols = slice(c * piece, (c + 1) * piece)
        teacher[:, cols] = (teacher[:, cols].astype(F32) * scale * gain_ref[:, cols]).astype(BF16)
    in_rows = width // peers
    if studT.shape[1] == in_rows and (width // 7) % 128 == 0:
        step = width // 7
        for c in range(7):
            turn = student[:, c * step:(c + 1) * step].T
            for r in range(0, step, SLOT):
                d, low = divmod(c * step + r, in_rows)
                studT[d, low:low + SLOT, :] = turn[r:r + SLOT, :]
    else:
        studT[...] = jnp.zeros_like(studT)
        flat = student[...].astype(F32).T
        for d in range(peers):
            studT[d, :in_rows, :] = flat[d * in_rows:(d + 1) * in_rows, :].astype(BF16)
    col = iota((slots, all_slots), 1)
    packed = ones_where((iota((slots, all_slots), 0) == (col >> 4) * cap + (col & 15)) & ((col & 15) < cap))
    row = iota((all_slots, slots), 0)
    spread = ones_where((iota((all_slots, slots), 1) == (row >> 4) * cap + (row & 15)) & ((row & 15) < cap))
    out_rows = rank_in // peers
    places, plan = out_plan(out_rows)
    row = iota((all_slots, 1), 0)
    pos, entry = row // SLOT, row % SLOT
    rest = pos % half
    dest = ((rest % depth) * 4 + (rest // depth) * 2 + pos // half) ^ me
    outsel = [
        ones_where(
            (iota((all_slots, rank_in), 1) == dest * out_rows + (lo + entry - off))
            & (entry >= off) & (entry < off + n)
        )
        for lo, n, off in places
    ]
    loads[3].wait()
    wait_all(*go)

    latents = nn(packed, rcv[...].reshape(all_slots, lat.shape[1]))[:, :rank_in].astype(BF16)
    grad = jnp.zeros((slots, rank_in), F32)
    total = jnp.zeros((slots, 1), F32)
    for c in range(8):
        cols = slice(c * piece, (c + 1) * piece)
        diff = nn(latents, pout[:, cols]) - teacher[:, cols].astype(F32)
        total += jnp.sum(diff * diff, axis=1, keepdims=True)
        e = (diff * factor).astype(BF16)
        err[:, cols] = e
        grad += nt(e, pout[:, cols])
    ret[:, :rank_in] = grad.astype(BF16)
    ret[:, rank_in:rank_in + 1] = (total * (1.0 / window)).astype(BF16)
    snd2[...] = nn(spread, ret[...]).astype(BF16).reshape(snd2.shape)
    back = (snd2, rcv2, y_ss, y_rs)
    start_all(*back)
    rcv2[me] = snd2[me]

    jobs = len(plan)

    def send(src, dst, ss, rs, bits):
        return pltpu.make_async_remote_copy(
            src_ref=src, dst_ref=dst, send_sem=ss, recv_sem=rs,
            device_id={"dp": flip(me, bits)}, device_id_type=MESH,
        )

    def refs(j):
        if j < jobs:
            return [r.at[j] for r in (ga_s, ga_r, gacc, gb_s, gb_r, gc_s, gc_r)]
        return [ia_s, ia_r, iacc, ib_s, ib_r, ic_s, ic_r]

    def copy_a(j):
        r = refs(j)
        return send(r[0], r[1], a_ss.at[j], a_rs.at[j], 1)

    def copy_b(j):
        r = refs(j)
        return send(r[3], r[4], b_ss.at[j], b_rs.at[j], 2)

    def copy_c(j, z):
        r = refs(j)
        return send(r[5].at[z - 1], r[6].at[z - 1], c_ss.at[j, z], c_rs.at[j, z], 4 * z)

    def after_a(j):
        a_s, a_r, acc, b_s, b_r, c_s, c_r = refs(j)
        copy_a(j).wait_recv()
        for h in range(depth, half):
            b_s[h - depth] = (acc[h] + a_r[h].astype(F32)).astype(BF16)
        copy_b(j).start()
        for h in range(depth):
            acc[h] = acc[h] + a_r[h].astype(F32)

    def after_b(j):
        a_s, a_r, acc, b_s, b_r, c_s, c_r = refs(j)
        copy_b(j).wait_recv()
        for z in range(depth - 1, 0, -1):
            c_s[z - 1] = (acc[z] + b_r[z].astype(F32)).astype(BF16)
            copy_c(j, z).start()
        acc[0] = acc[0] + b_r[0].astype(F32)

    def after_c(j):
        a_s, a_r, acc, b_s, b_r, c_s, c_r = refs(j)
        total = acc[0]
        for z in range(1, depth):
            copy_c(j, z).wait_recv()
            total += c_r[z - 1].astype(F32)
        return total

    turned = [nt(s, latents).astype(BF16) for s in outsel]
    chunk = window // 4
    for j, terms in enumerate(plan):
        for first in (half * SLOT, 0):
            part = sum(
                nn(turned[p][first:first + half * SLOT], err[:, s * chunk:(s + 1) * chunk])
                for s, p in terms
            )
            if first:
                ga_s[j] = part.astype(BF16).reshape(half, SLOT, chunk)
                copy_a(j).start()
            else:
                gacc[j] = part.reshape(half, SLOT, chunk)
    after_a(0)

    wait_all(*back)
    picked = tn(pick, rcv2[...].reshape(all_slots, lat.shape[1]))
    last = picked[:, 128:]
    loss_ref[...] = last.T[rank_in - 128:rank_in - 127, :].astype(BF16)
    lane = iota((tok, 128), 1) < 64
    right = jnp.where(lane, last, pltpu.roll(last, 64, 1)).astype(BF16)
    left = picked[:, :128].astype(BF16)
    whole_rows = studT.shape[1]
    split = whole_rows // 2
    low = iota((split, 128), 1) < 64
    for dc in (1, 0):
        for h in range(half):
            source = studT[flip(me, (h % depth) * 4 + (h // depth) * 2 + dc)]
            one = nn(source, left)
            two = nn(source, right)
            two = jnp.where(low, two[:split], two[split:])
            if dc:
                ia_s[h, :whole_rows, :] = one.astype(BF16)
                ia_s[h, whole_rows:, :] = two.astype(BF16)
            else:
                iacc[h, :whole_rows, :] = one
                iacc[h, whole_rows:, :] = two
        if dc:
            copy_a(jobs).start()
    for j in range(1, jobs + 1):
        after_a(j)
    for j in range(jobs + 1):
        after_b(j)
    for j in range(jobs):
        out_sum[j] = after_c(j)
    in_sum[...] = after_c(jobs)

    drain_all(*go)
    drain_all(*back)
    for j in range(jobs + 1):
        copy_a(j).wait_send()
        copy_b(j).wait_send()
        for z in range(1, depth):
            copy_c(j, z).wait_send()


def unpack(out_rows, in_sum, out_sum, loss_in, gin_ref, gout_ref, loss_ref):
    places, plan = out_plan(out_rows)
    chunk = out_sum.shape[2]
    for j, terms in enumerate(plan):
        for s, p in terms:
            lo, n, off = places[p]
            gout_ref[lo:lo + n, s * chunk:(s + 1) * chunk] = out_sum[j, off:off + n, :]
    rank, in_rows = gin_ref.shape
    whole = in_sum.shape[0] * 2 // 3
    split = whole // 2
    gin_ref[:128, :] = in_sum[:whole, :].T[:, :in_rows]
    two = in_sum[whole:, :].T
    gin_ref[128:, :split] = two[:64]
    gin_ref[128:, split:] = two[64:, :in_rows - split]
    loss_ref[...] = loss_in[...]


def local(peers, student_hidden, teacher_rows, teacher_of_row, teacher_gain, proj_in, proj_out):
    tok, width = student_hidden.shape
    slots, window = teacher_rows.shape
    rank = proj_in.shape[1]
    padded = (rank // 128 + 1) * 128
    half, depth = peers // 2, peers // 4
    in_rows = width // peers
    in_pad = -(-in_rows // 32) * 32
    block = in_pad * 3 // 2
    out_rows = rank // peers
    jobs = len(out_plan(out_rows)[1])
    chunk = window // 4
    last = max(depth - 1, 1)
    vmem, dma = pltpu.VMEM, pltpu.SemaphoreType.DMA
    scratch = [
        vmem((tok, width), BF16), vmem((slots, window), BF16), vmem((rank, width), BF16),
        vmem((rank, window), BF16), dma((4,)),
        vmem((tok, padded), BF16),
        *[vmem((peers, SLOT, padded), BF16)] * 4,
        vmem((peers, in_pad, tok), BF16), vmem((slots, window), BF16), vmem((slots, padded), BF16),
    ]
    for lead, tile in (((jobs,), (SLOT, chunk)), ((), (block, 128))):
        scratch += [
            vmem((*lead, half, *tile), BF16), vmem((*lead, half, *tile), BF16),
            vmem((*lead, half, *tile), F32),
            vmem((*lead, depth, *tile), BF16), vmem((*lead, depth, *tile), BF16),
            vmem((*lead, last, *tile), BF16), vmem((*lead, last, *tile), BF16),
        ]
    scratch += [dma((peers,))] * 4 + [dma((jobs + 1,))] * 4 + [dma((jobs + 1, depth))] * 2
    anywhere, inside = pl.BlockSpec(memory_space=pl.ANY), pl.BlockSpec(memory_space=pltpu.VMEM)
    cfg = dict(peers=peers, cap=slots // peers, rank=rank)
    in_sum, out_sum, row_loss = pl.pallas_call(
        functools.partial(kernel, cfg),
        out_shape=(
            jax.ShapeDtypeStruct((block, 128), F32),
            jax.ShapeDtypeStruct((jobs, SLOT, chunk), F32),
            jax.ShapeDtypeStruct((1, tok), BF16),
        ),
        in_specs=[anywhere, anywhere, inside, inside, anywhere, anywhere],
        out_specs=(inside, inside, inside),
        scratch_shapes=scratch,
        compiler_params=pltpu.CompilerParams(
            collective_id=0, has_side_effects=True, vmem_limit_bytes=56 * 2**20
        ),
    )(
        student_hidden, teacher_rows, teacher_of_row.reshape(1, tok),
        teacher_gain.reshape(1, window), proj_in.T, proj_out,
    )
    grad_in, grad_out, row_loss = pl.pallas_call(
        functools.partial(unpack, out_rows),
        out_shape=(
            jax.ShapeDtypeStruct((rank, in_rows), F32),
            jax.ShapeDtypeStruct((out_rows, window), F32),
            jax.ShapeDtypeStruct((1, tok), BF16),
        ),
    )(in_sum, out_sum, row_loss)
    return grad_in.T, grad_out, row_loss.reshape(tok)


def solution(mesh):
    rows = P(("parts", "dp"), None)
    return jax.shard_map(
        functools.partial(local, mesh.shape["dp"]),
        mesh=mesh,
        in_specs=(rows, rows, rows, P(), P(), P()),
        out_specs=(rows, rows, P(("parts", "dp"))),
        check_vma=False,
    )
```

```python
import functools
import math

import jax
import jax.numpy as jnp
from jax import lax
from jax.experimental import pallas as pl
from jax.experimental.pallas import tpu as pltpu
from jax.sharding import PartitionSpec as P

F32 = jnp.float32
BF16 = jnp.bfloat16
MESH = pl.DeviceIdType.MESH
SLOT = 16


def flip(index, bits):
    weight = 1
    while bits:
        if bits % 2:
            index = index + (1 - 2 * ((index // weight) % 2)) * weight
        bits //= 2
        weight *= 2
    return index


def nt(left, right):
    return lax.dot_general(left, right, (((1,), (1,)), ((), ())), preferred_element_type=F32)


def tn(left, right):
    return lax.dot_general(left, right, (((0,), (0,)), ((), ())), preferred_element_type=F32)


def nn(left, right):
    return jnp.dot(left, right, preferred_element_type=F32)


def ones_where(condition):
    return jnp.where(condition, 1.0, 0.0).astype(BF16)


def iota(shape, dim):
    return lax.broadcasted_iota(jnp.int32, shape, dim)


def out_plan(rows):
    if rows == 12:
        places = [(0, 12, 0)] + [(4 * q, 4, 12) for q in range(3)]
        return places, [[(q, 0), (3, q + 1)] for q in range(3)]
    if 4 * rows <= SLOT:
        return [(0, rows, rows * s) for s in range(4)], [[(s, s) for s in range(4)]]
    return [(0, rows, 0)], [[(s, 0)] for s in range(4)]


def job_orders(jobs, stages):
    rising = tuple(1 << i for i in range(stages))
    other = rising[:1] + rising[2:3] + rising[1:2] + rising[3:]
    orders = [rising] * (jobs + 3)
    orders[jobs + 1] = other
    if jobs > 1:
        orders[1] = other
    return orders


def kernel(
    cfg, student_hbm, teacher_hbm, owner_ref, gain_ref, pin_hbm, pout_hbm,
    in_sum, out_sum, loss_ref,
    student, teacher, pin, pout, load_sem,
    lat, snd, rcv, snd2, rcv2, studT, err, ret,
    g_out, g_into, g_acc, i_out, i_into, i_acc,
    x_ss, x_rs, y_ss, y_rs, j_ss, j_rs,
):
    peers, cap, rank_in = cfg["peers"], cfg["cap"], cfg["rank"]
    half, stages = peers // 2, peers.bit_length() - 1
    tok, width = student.shape
    slots, window = teacher.shape
    all_slots = peers * SLOT
    factor = 1.0 / math.sqrt(tok * peers)
    me = lax.axis_index("dp")

    loads = [
        pltpu.make_async_copy(src, dst, load_sem.at[n])
        for n, (src, dst) in enumerate(
            [(student_hbm, student), (pin_hbm, pin), (teacher_hbm, teacher), (pout_hbm, pout)]
        )
    ]
    for load in loads:
        load.start()

    barrier = pltpu.get_barrier_semaphore()

    @pl.loop(1, peers)
    def _(k):
        pl.semaphore_signal(
            barrier, inc=1, device_id={"dp": lax.rem(me + k, peers)}, device_id_type=MESH
        )

    owner = owner_ref[...]
    onehot = ones_where(owner == iota((peers, tok), 0))
    upto = ones_where(iota((tok, tok), 0) <= iota((tok, tok), 1))
    rank = jnp.sum(nn(onehot, upto) * onehot.astype(F32), axis=0, keepdims=True) - 1.0
    place = owner * SLOT + rank.astype(jnp.int32)
    pick = ones_where(place == iota((all_slots, tok), 0))

    lat[...] = jnp.zeros_like(lat)
    ret[...] = jnp.zeros_like(ret)
    loads[0].wait()
    loads[1].wait()
    lat[:, :rank_in] = nt(student[...], pin[...]).astype(BF16)
    snd[...] = nn(pick, lat[...]).astype(BF16).reshape(snd.shape)

    def each_peer(step):
        if peers <= 16:
            for k in sorted(range(1, peers), key=lambda k: -min(k, peers - k)):
                step(k)
        else:
            pl.loop(1, peers)(step)

    def exchange(k, out, into, ss, rs):
        peer = lax.rem(me + k, peers)
        return pltpu.make_async_remote_copy(
            src_ref=out.at[peer], dst_ref=into.at[me], send_sem=ss.at[k], recv_sem=rs.at[k],
            device_id={"dp": peer}, device_id_type=MESH,
        )

    def arrival(k, out, into, ss, rs):
        source = lax.rem(me - k + peers, peers)
        return pltpu.make_async_remote_copy(
            src_ref=out.at[source], dst_ref=into.at[source], send_sem=ss.at[k], recv_sem=rs.at[k],
            device_id={"dp": source}, device_id_type=MESH,
        )

    def start_all(*refs):
        each_peer(lambda k: exchange(k, *refs).start())

    def wait_all(*refs):
        each_peer(lambda k: arrival(k, *refs).wait_recv())

    def drain_all(*refs):
        each_peer(lambda k: exchange(k, *refs).wait_send())

    loads[2].wait()
    piece = window // 8
    total = jnp.zeros((slots, 1), F32)
    for c in range(8):
        v = teacher[:, c * piece:(c + 1) * piece].astype(F32)
        total += jnp.sum(v * v, axis=1, keepdims=True)
    scale = lax.rsqrt(total * (1.0 / window) + 1e-06)
    for c in range(8):
        cols = slice(c * piece, (c + 1) * piece)
        teacher[:, cols] = (teacher[:, cols].astype(F32) * scale * gain_ref[:, cols]).astype(BF16)
    go = (snd, rcv, x_ss, x_rs)
    pl.semaphore_wait(barrier, peers - 1)
    start_all(*go)
    rcv[me] = snd[me]
    in_rows = width // peers
    if studT.shape[1] == in_rows and (width // 7) % 128 == 0:
        step = width // 7
        for c in range(7):
            turn = student[:, c * step:(c + 1) * step].T
            for r in range(0, step, SLOT):
                d, low = divmod(c * step + r, in_rows)
                studT[d, low:low + SLOT, :] = turn[r:r + SLOT, :]
    else:
        studT[...] = jnp.zeros_like(studT)
        flat = student[...].astype(F32).T
        for d in range(peers):
            studT[d, :in_rows, :] = flat[d * in_rows:(d + 1) * in_rows, :].astype(BF16)
    col = iota((slots, all_slots), 1)
    packed = ones_where((iota((slots, all_slots), 0) == (col >> 4) * cap + (col & 15)) & ((col & 15) < cap))
    row = iota((all_slots, slots), 0)
    spread = ones_where((iota((all_slots, slots), 1) == (row >> 4) * cap + (row & 15)) & ((row & 15) < cap))
    out_rows = rank_in // peers
    places, plan = out_plan(out_rows)
    row = iota((all_slots, 1), 0)
    pos, entry = row // SLOT, row % SLOT
    jobs = len(plan)
    orders = job_orders(jobs, stages)
    outsel = {}
    for j, terms in enumerate(plan):
        dest = sum(((pos >> (stages - 1 - i)) & 1) * bit for i, bit in enumerate(orders[j])) ^ me
        for _, p in terms:
            lo, n, off = places[p]
            if (orders[j], p) not in outsel:
                outsel[orders[j], p] = ones_where(
                    (iota((all_slots, rank_in), 1) == dest * out_rows + (lo + entry - off))
                    & (entry >= off) & (entry < off + n)
                )
    loads[3].wait()
    wait_all(*go)

    latents = nn(packed, rcv[...].reshape(all_slots, lat.shape[1]))[:, :rank_in].astype(BF16)
    turned = {key: nt(sel, latents).astype(BF16) for key, sel in outsel.items()}

    def refs(j):
        if j < jobs:
            return g_out.at[j], g_into.at[j], g_acc.at[j]
        return i_out.at[j - jobs], i_into.at[j - jobs], i_acc.at[j - jobs]

    def copy(j, stage):
        out, into, _ = refs(j)
        count = peers >> (stage + 1)
        return pltpu.make_async_remote_copy(
            src_ref=out.at[pl.ds(count, count)], dst_ref=into.at[pl.ds(count, count)],
            send_sem=j_ss.at[j, stage], recv_sem=j_rs.at[j, stage],
            device_id={"dp": flip(me, orders[j][stage])}, device_id_type=MESH,
        )

    def advance(j, stage):
        out, into, acc = refs(j)
        copy(j, stage).wait_recv()
        count = peers >> (stage + 1)
        kept = count // 2
        if kept:
            for h in range(kept, count):
                out[h] = (acc[h] + into[count + h].astype(F32)).astype(BF16)
            copy(j, stage + 1).start()
        for h in range(max(kept, 1)):
            acc[h] = acc[h] + into[count + h].astype(F32)

    grad = jnp.zeros((slots, rank_in), F32)
    total = jnp.zeros((slots, 1), F32)
    chunk = window // 4
    ready, started = set(), []
    for quarter in (3, 0, 1, 2):
        for c in (2 * quarter, 2 * quarter + 1):
            cols = slice(c * piece, (c + 1) * piece)
            diff = nn(latents, pout[:, cols]) - teacher[:, cols].astype(F32)
            total += jnp.sum(diff * diff, axis=1, keepdims=True)
            e = (diff * factor).astype(BF16)
            err[:, cols] = e
            grad += nt(e, pout[:, cols])
        ready.add(quarter)
        for j, terms in enumerate(plan):
            if j in started or not ready.issuperset(q for q, _ in terms):
                continue
            for first in (half * SLOT, 0):
                part = sum(
                    nn(turned[orders[j], p][first:first + half * SLOT], err[:, q * chunk:(q + 1) * chunk])
                    for q, p in terms
                )
                if first:
                    g_out[j, half:] = part.astype(BF16).reshape(half, SLOT, chunk)
                    copy(j, 0).start()
                else:
                    g_acc[j] = part.reshape(half, SLOT, chunk)
            if started:
                advance(started[-1], 0)
            started.append(j)
    ret[:, :rank_in] = grad.astype(BF16)
    ret[:, rank_in:rank_in + 1] = (total * (1.0 / window)).astype(BF16)
    snd2[...] = nn(spread, ret[...]).astype(BF16).reshape(snd2.shape)
    back = (snd2, rcv2, y_ss, y_rs)
    start_all(*back)
    rcv2[me] = snd2[me]
    advance(started[-1], 0)

    wait_all(*back)
    picked = tn(pick, rcv2[...].reshape(all_slots, lat.shape[1]))
    last = picked[:, 128:]
    loss_ref[...] = last.T[rank_in - 128:rank_in - 127, :].astype(BF16)
    lane = iota((tok, 128), 1) < 64
    right = jnp.where(lane, last, pltpu.roll(last, 64, 1)).astype(BF16)
    left = picked[:, :128].astype(BF16)
    whole_rows = studT.shape[1]
    split = whole_rows // 2
    low = iota((split, 128), 1) < 64
    early = [(j, 1) for j in range(min(jobs, 2))]
    for j, t in early:
        advance(j, t)
    for j in range(jobs, jobs + 3):
        out, _, acc = refs(j)
        for core in (1, 0):
            for h in range(half):
                bits = orders[j][0] * core + sum(
                    bit for i, bit in enumerate(orders[j]) if i and (h >> (stages - 1 - i)) & 1
                )
                source = studT[flip(me, bits)]
                if j < jobs + 2:
                    block = nn(source[(j - jobs) * split:(j - jobs + 1) * split], left)
                else:
                    block = nn(source, right)
                    block = jnp.where(low, block[:split], block[split:])
                if core:
                    out[half + h] = block.astype(BF16)
                else:
                    acc[h] = block
            if core:
                copy(j, 0).start()
    steps = [(j + 3 * t, j, t) for j in range(jobs + 3) for t in range(stages) if j >= jobs or t > 0]
    for _, j, t in sorted(steps):
        if (j, t) not in early:
            advance(j, t)
    for j in range(jobs):
        out_sum[j] = g_acc[j, 0]
    for j in range(3):
        in_sum[j * split:(j + 1) * split, :] = i_acc[j, 0]

    drain_all(*go)
    drain_all(*back)
    for j in range(jobs + 3):
        for t in range(stages):
            copy(j, t).wait_send()


def unpack(out_rows, in_sum, out_sum, loss_in, gin_ref, gout_ref, loss_ref):
    places, plan = out_plan(out_rows)
    chunk = out_sum.shape[2]
    for j, terms in enumerate(plan):
        for s, p in terms:
            lo, n, off = places[p]
            gout_ref[lo:lo + n, s * chunk:(s + 1) * chunk] = out_sum[j, off:off + n, :]
    rank, in_rows = gin_ref.shape
    whole = in_sum.shape[0] * 2 // 3
    split = whole // 2
    gin_ref[:128, :] = in_sum[:whole, :].T[:, :in_rows]
    two = in_sum[whole:, :].T
    gin_ref[128:, :split] = two[:64]
    gin_ref[128:, split:] = two[64:, :in_rows - split]
    loss_ref[...] = loss_in[...]


def local(peers, student_hidden, teacher_rows, teacher_of_row, teacher_gain, proj_in, proj_out):
    tok, width = student_hidden.shape
    slots, window = teacher_rows.shape
    rank = proj_in.shape[1]
    padded = (rank // 128 + 1) * 128
    half = peers // 2
    in_rows = width // peers
    in_pad = -(-in_rows // 32) * 32
    block = in_pad * 3 // 2
    out_rows = rank // peers
    jobs = len(out_plan(out_rows)[1])
    chunk = window // 4
    vmem, dma = pltpu.VMEM, pltpu.SemaphoreType.DMA
    scratch = [
        vmem((tok, width), BF16), vmem((slots, window), BF16), vmem((rank, width), BF16),
        vmem((rank, window), BF16), dma((4,)),
        vmem((tok, padded), BF16),
        *[vmem((peers, SLOT, padded), BF16)] * 4,
        vmem((peers, in_pad, tok), BF16), vmem((slots, window), BF16), vmem((slots, padded), BF16),
    ]
    for lead, tile in ((jobs, (SLOT, chunk)), (3, (in_pad // 2, 128))):
        scratch += [vmem((lead, peers, *tile), BF16)] * 2 + [vmem((lead, half, *tile), F32)]
    scratch += [dma((peers,))] * 4 + [dma((jobs + 3, peers.bit_length() - 1))] * 2
    anywhere, inside = pl.BlockSpec(memory_space=pl.ANY), pl.BlockSpec(memory_space=pltpu.VMEM)
    cfg = dict(peers=peers, cap=slots // peers, rank=rank)
    in_sum, out_sum, row_loss = pl.pallas_call(
        functools.partial(kernel, cfg),
        out_shape=(
            jax.ShapeDtypeStruct((block, 128), F32),
            jax.ShapeDtypeStruct((jobs, SLOT, chunk), F32),
            jax.ShapeDtypeStruct((1, tok), BF16),
        ),
        in_specs=[anywhere, anywhere, inside, inside, anywhere, anywhere],
        out_specs=(inside, inside, inside),
        scratch_shapes=scratch,
        compiler_params=pltpu.CompilerParams(
            collective_id=0, has_side_effects=True, vmem_limit_bytes=56 * 2**20
        ),
    )(
        student_hidden, teacher_rows, teacher_of_row.reshape(1, tok),
        teacher_gain.reshape(1, window), proj_in.T, proj_out,
    )
    grad_in, grad_out, row_loss = pl.pallas_call(
        functools.partial(unpack, out_rows),
        out_shape=(
            jax.ShapeDtypeStruct((rank, in_rows), F32),
            jax.ShapeDtypeStruct((out_rows, window), F32),
            jax.ShapeDtypeStruct((1, tok), BF16),
        ),
    )(in_sum, out_sum, row_loss)
    return grad_in.T, grad_out, row_loss.reshape(tok)


def solution(mesh):
    rows = P(("parts", "dp"), None)
    return jax.shard_map(
        functools.partial(local, mesh.shape["dp"]),
        mesh=mesh,
        in_specs=(rows, rows, rows, P(), P(), P()),
        out_specs=(rows, rows, P(("parts", "dp"))),
        check_vma=False,
    )
```
